512 devices in a mesh: dp: 16 (over x, z_hi), seq: 32 (over y, z_lo, core).
Axes of the slice: x: 4, y: 4, z: 16 (z_hi: 4, z_lo: 4; z = z_hi * 4 + z_lo), core: 2. Of those that a mesh axis runs over, the one named last changes fastest.
Arguments:
- queries: bfloat16 [16, 4096, 4096], P('dp', 'seq'), may hold values from -6 to 6
- products: bfloat16 [16, 4096, 4096], P('dp', 'seq'), may hold values from -6 to 6
- packed_grad: bfloat16 [16, 4096, 4096], P('dp', 'seq'), may hold values from -6 to 6
- packed_target: int32 [16, 4096], P('dp', 'seq'), may hold values from 0 to 4095, as said below
- short_filter: bfloat16 [3, 4096], replicated, may hold values from -3.5 to 3.5
- medium_filter: bfloat16 [128, 256], replicated, may hold values from -0.5 to 0.5
Outputs:
- input_grad: bfloat16 [16, 4096, 4096], P('dp', 'seq')
- medium_grad: float32 [128, 256], replicated
- short_grad: float32 [3, 4096], replicated
The draws below stay inside these ranges and needn't reach their ends.
Inputs may be any that keep to these rules, and one draw needn't show every extreme that they name: `packed_target`: for each sequence a permutation of its positions. The 128 packed rows of one device hold at most 8 positions of any one device's 128 positions, and exactly 8 for some pairs of devices in every draw.
All inputs are finite; a program needn't handle non-finite values.
Results may differ from the reference program's by a relative error of at most 0.011.
Values may be sent and summed in bfloat16 or wider, within the bound.
No kernel may reach another device: no remote copies, remote signals or barrier semaphores. Data moves between devices by JAX's collectives and lax.ppermute only.
A program may use at most 128 MiB of HBM per device.

```python
import math
import jax
import jax.numpy as jnp
from jax import lax

D = 4096
GROUPS = 256
TAPS = 128
SHORT = 3
TOK_DEV = 128
LENGTH = 4096
BATCH = 16


def route_sequence(key, seq_length, block_rows):
    shards = seq_length // block_rows
    base = block_rows // shards
    keys = jax.random.split(key, 4)
    sigma = jax.random.permutation(keys[0], shards)
    amount = jax.random.randint(keys[1], (), 1, base)
    source = jnp.arange(shards)

    def onehot(index):
        return (sigma[index][:, None] == source[None, :]).astype(jnp.int32)
    counts = base + base * onehot(source) - amount * onehot((source + 1) % shards) - (base - amount) * onehot((source + 2) % shards)
    bounds = jnp.cumsum(counts, axis=0)
    slots = jnp.arange(block_rows)
    sender = jnp.sum((bounds[:, :, None] <= slots[None, None, :]).astype(jnp.int32), axis=0)
    shuffle_keys = jax.random.split(keys[2], shards)
    shuffles = jax.vmap(partial_perm(block_rows))(shuffle_keys)
    positions = source[:, None] * block_rows + shuffles
    tiebreak = jax.random.permutation(keys[3], seq_length)
    scores = sender.reshape(-1) * seq_length + tiebreak
    arrange = jnp.argsort(scores)
    return positions.reshape(-1)[arrange].astype(jnp.int32)


def partial_perm(count):

    def permute(key):
        return jax.random.permutation(key, count)
    return permute


def draw_packed_target(key, part):
    key = jax.random.fold_in(key, 11)
    keys = jax.random.split(key, BATCH)
    rows_list = [route_sequence(keys[index], LENGTH, TOK_DEV) for index in range(BATCH)]
    return jnp.stack(rows_list).astype(jnp.int32)


def steps_of(key, shape, cuts, least, high):
    gain, own = 1.0, jax.random.fold_in(key, 6)
    for dim, blocks in cuts:
        draws = jnp.exp(jax.random.uniform(jax.random.fold_in(own, dim), (blocks,), jnp.float32, least / len(cuts), high / len(cuts)))
        gain = gain * jnp.repeat(draws, shape[dim] // blocks).reshape([-1 if axis == dim else 1 for axis in range(len(shape))])
    return gain


def noise(own_key, dims, scale, reach, cuts=(), kind=jnp.bfloat16):
    result = scale * jax.random.normal(own_key, dims, jnp.float32)
    if cuts:
        result = result * steps_of(own_key, dims, cuts, -0.22, 0.18)
    return jnp.clip(result, -reach, reach).astype(kind)


def setup_inputs(seed: int = 0) -> dict:
    arg_keys = jax.random.split(jax.random.key(seed), 7)
    queries = noise(arg_keys[0], (BATCH, LENGTH, D), 1.0, 6.0, ((0, 16), (1, 32)))
    products = noise(arg_keys[1], (BATCH, LENGTH, D), 1.0, 6.0, ((0, 16), (1, 32)))
    packed_grad = noise(arg_keys[2], (BATCH, LENGTH, D), 1.0, 6.0, ((0, 16), (1, 32)))
    packed_target = draw_packed_target(jax.random.fold_in(arg_keys[6], 71), 0)
    short_filter = noise(arg_keys[4], (SHORT, D), SHORT ** -0.5, 3.5)
    medium_filter = noise(arg_keys[5], (TAPS, GROUPS), TAPS ** -0.5, 0.5)
    return dict(queries=queries, products=products, packed_grad=packed_grad, packed_target=packed_target, short_filter=short_filter, medium_filter=medium_filter)


def shifted(values, offset):
    if offset == 0:
        return values
    front = jnp.zeros((offset,) + values.shape[1:], values.dtype)
    return jnp.concatenate([front, values[:values.shape[0] - offset]], axis=0)

def reference(queries, products, packed_grad, packed_target, short_filter, medium_filter):
    seq_length = queries.shape[1]
    channels = queries.shape[2]
    tap_count = medium_filter.shape[0]
    group_count = medium_filter.shape[1]
    per_group = channels // group_count
    short_count = short_filter.shape[0]
    fft_size = int(2 ** math.ceil(math.log2(seq_length + tap_count)))
    half_size = fft_size // 2 + 1
    inverse = jnp.argsort(packed_target, axis=1).astype(jnp.int32)
    routed = jnp.take_along_axis(packed_grad, inverse[:, :, None], axis=1)
    filter_spec = jnp.fft.rfft(medium_filter.astype(jnp.float32), n=fft_size, axis=0)
    filter_wide = jnp.repeat(filter_spec, per_group, axis=1)
    short_wide = short_filter.astype(jnp.float32)

    def per_sequence(items):
        query, product, gradient = items
        query_f = query.astype(jnp.float32)
        smoothed = sum((short_wide[offset] * shifted(query_f, offset) for offset in range(short_count)))
        product_spec = jnp.fft.rfft(product.astype(jnp.float32), n=fft_size, axis=0)
        hidden = jnp.fft.irfft(product_spec * filter_wide, n=fft_size, axis=0)[:seq_length]
        grad_f = gradient.astype(jnp.float32)
        hidden_grad = (grad_f * smoothed).astype(jnp.bfloat16)
        hidden_grad = lax.optimization_barrier(hidden_grad)
        smooth_grad = grad_f * hidden
        grad_spec = jnp.fft.rfft(hidden_grad.astype(jnp.float32), n=fft_size, axis=0)
        input_grad = jnp.fft.irfft(grad_spec * jnp.conj(filter_wide), n=fft_size, axis=0)[:seq_length]
        cross = (grad_spec * jnp.conj(product_spec)).reshape(half_size, group_count, per_group).sum(axis=2)
        lagged = jnp.fft.irfft(cross, n=fft_size, axis=0)[:tap_count]
        short_terms = jnp.stack([lax.optimization_barrier(jnp.sum(smooth_grad * shifted(query_f, offset), axis=0)) for offset in range(short_count)])
        return (input_grad.astype(jnp.bfloat16), lagged, short_terms)
    input_grad, lagged, short_terms = lax.map(per_sequence, (queries, products, routed))
    batch_count = queries.shape[0]
    medium_grad = lax.optimization_barrier(jnp.sum(lagged, axis=0)) / math.sqrt(batch_count * seq_length * per_group)
    short_grad = lax.optimization_barrier(jnp.sum(short_terms, axis=0)) / math.sqrt(batch_count * seq_length)
    return (input_grad, medium_grad, short_grad)
```

```python
import math

import jax
import jax.numpy as jnp
import numpy as np
from jax import lax
from jax.experimental import pallas as pl
from jax.experimental.pallas import tpu as pltpu
from jax.sharding import PartitionSpec as P

TILE = 512
LANES = 128
BLOCK_ROWS = 16
MIB = 1024 * 1024


def split(value):
    high = value.astype(jnp.bfloat16)
    low = (value - high.astype(jnp.float32)).astype(jnp.bfloat16)
    return high, low


def wave_table(rows):
    size = 2 * rows
    phase = (np.arange(size)[None, :] * (2 * np.arange(rows)[:, None] + 1)) % (2 * size)
    angle = phase * (math.pi / size)
    return np.concatenate([np.cos(angle), -np.sin(angle)], axis=0)


def halves(table):
    high = table.astype(jnp.bfloat16)
    low = (table - high.astype(np.float64)).astype(jnp.bfloat16)
    return jnp.asarray(high), jnp.asarray(low)


def mm(left, right):
    return jnp.dot(left, right, preferred_element_type=jnp.float32)


def forward(high, low, value):
    return mm(high, value) + mm(low, value)


def backward(high, low, value):
    top, rest = split(value)
    return mm(high, top) + (mm(low, top) + mm(high, rest))


def halved(spec):
    half = spec.shape[0] // 2
    return spec[:half], spec[half:]


def filter_spec(taps, high, low, per_group):
    tap_count, group_count = taps.shape
    channel = lax.broadcasted_iota(jnp.int32, (group_count, TILE), 1) + pl.program_id(0) * TILE
    group = lax.broadcasted_iota(jnp.int32, (group_count, TILE), 0)
    first = group * per_group
    expand = ((channel >= first) & (channel < first + per_group)).astype(jnp.bfloat16)
    wide = mm(taps, expand).astype(jnp.bfloat16)
    return forward(high[:, :tap_count], low[:, :tap_count], wide)


def delayed(query, tail, steps):
    moved = pltpu.roll(query, steps, 0)
    row = lax.broadcasted_iota(jnp.int32, query.shape, 0)
    for index in range(steps):
        source = tail.shape[0] - steps + index
        moved = jnp.where(row == index, tail[source : source + 1], moved)
    return moved


def pack_kernel(capacity, target_ref, grad_ref, out_ref):
    rows, channels = grad_ref.shape
    slots = out_ref.shape[0]
    wide = jnp.broadcast_to(target_ref[...].astype(jnp.float32), (rows, rows))
    across = wide.astype(jnp.int32)
    down = wide.T.astype(jnp.int32)
    upper = lax.broadcasted_iota(jnp.int32, (rows, rows), 0)
    right = lax.broadcasted_iota(jnp.int32, (rows, rows), 1)
    owner = lax.div(across, rows)
    earlier = (owner == lax.div(down, rows)) & (upper < right)
    rank = jnp.sum(earlier.astype(jnp.float32), axis=0, keepdims=True).astype(jnp.int32)
    slot = owner[:1] * capacity + rank
    placing = (lax.broadcasted_iota(jnp.int32, (slots, rows), 0) == slot).astype(jnp.bfloat16)
    landing = (lax.rem(down, rows) == right).astype(jnp.bfloat16)
    for start in range(0, channels, TILE):
        out_ref[:, start : start + TILE] = mm(placing, grad_ref[:, start : start + TILE]).astype(
            jnp.bfloat16
        )
    out_ref[:, channels:] = mm(placing, landing).astype(jnp.bfloat16)


def early_kernel(
    per_group,
    query_ref,
    tail_ref,
    own_ref,
    prev_ref,
    short_ref,
    taps_ref,
    fh_ref,
    fl_ref,
    ih_ref,
    il_ref,
    smooth_ref,
    hidden_ref,
    spec_ref,
):
    rows = own_ref.shape[0]
    spec = forward(
        fh_ref[...], fl_ref[...], jnp.concatenate([prev_ref[...], own_ref[...]], axis=0)
    )
    spec_ref[...] = spec
    wave = filter_spec(taps_ref[...], fh_ref, fl_ref, per_group)
    sr, si = halved(spec)
    wr, wi = halved(wave)
    product = jnp.concatenate([sr * wr - si * wi, sr * wi + si * wr], axis=0)
    hidden_ref[...] = backward(ih_ref[rows:], il_ref[rows:], product)
    query = query_ref[...].astype(jnp.float32)
    tail = tail_ref[...].astype(jnp.float32)
    short = short_ref[...].astype(jnp.float32)
    total = short[0:1] * query
    for offset in range(1, short.shape[0]):
        total = total + short[offset : offset + 1] * delayed(query, tail, offset)
    smooth_ref[...] = total


def grad_kernel(
    per_group,
    short_count,
    land_ref,
    recv_ref,
    smooth_ref,
    hidden_ref,
    spec_ref,
    query_ref,
    tail_ref,
    fh_ref,
    fl_ref,
    ch_ref,
    cl_ref,
    hgrad_ref,
    sums_ref,
):
    rows = hgrad_ref.shape[0]
    groups = TILE // per_group
    routed = lax.dot_general(
        land_ref[...],
        recv_ref[...],
        (((0,), (0,)), ((), ())),
        preferred_element_type=jnp.float32,
    )
    hgrad = (routed * smooth_ref[...]).astype(jnp.bfloat16)
    hgrad_ref[...] = hgrad
    sgrad = routed * hidden_ref[...]
    query = query_ref[...].astype(jnp.float32)
    tail = tail_ref[...].astype(jnp.float32)
    terms = [jnp.sum(sgrad * query, axis=0, keepdims=True)]
    for offset in range(1, short_count):
        terms.append(jnp.sum(sgrad * delayed(query, tail, offset), axis=0, keepdims=True))
    terms.append(jnp.zeros((8 - short_count, TILE), jnp.float32))
    short_terms = jnp.concatenate(terms, axis=0)
    gr, gi = halved(forward(fh_ref[:, rows:], fl_ref[:, rows:], hgrad))
    pr, pi = halved(spec_ref[...])
    cross = jnp.concatenate([gr * pr + gi * pi, gi * pr - gr * pi], axis=0)
    first = lax.broadcasted_iota(jnp.int32, (groups, TILE), 0) * per_group
    channel = lax.broadcasted_iota(jnp.int32, (groups, TILE), 1)
    member = ((channel >= first) & (channel < first + per_group)).astype(jnp.bfloat16)
    dims = (((1,), (1,)), ((), ()))
    top, rest = split(cross)
    grouped = lax.dot_general(member, top, dims, preferred_element_type=jnp.float32)
    grouped += lax.dot_general(member, rest, dims, preferred_element_type=jnp.float32)
    top, rest = split(grouped)
    lagged = mm(top, ch_ref[...]) + (mm(top, cl_ref[...]) + mm(rest, ch_ref[...]))
    for part in range(TILE // LANES):
        sums_ref[part, :8] = lagged[8 * part : 8 * part + 8]
        sums_ref[part, 8:] = short_terms[:, part * LANES : (part + 1) * LANES]


def input_kernel(
    per_group, own_ref, next_ref, taps_ref, fh_ref, fl_ref, ih_ref, il_ref, out_ref
):
    rows = own_ref.shape[0]
    spec = forward(
        fh_ref[...], fl_ref[...], jnp.concatenate([own_ref[...], next_ref[...]], axis=0)
    )
    wave = filter_spec(taps_ref[...], fh_ref, fl_ref, per_group)
    gr, gi = halved(spec)
    wr, wi = halved(wave)
    product = jnp.concatenate([gr * wr + gi * wi, gi * wr - gr * wi], axis=0)
    out_ref[...] = backward(ih_ref[:rows], il_ref[:rows], product).astype(jnp.bfloat16)


def last_kernel(medium_scale, short_scale, sums_ref, medium_ref, short_ref):
    parts = sums_ref.shape[0]
    groups = medium_ref.shape[1]
    medium = sums_ref[:, :8, :].reshape(groups, LANES)
    medium_ref[...] = medium.T * medium_scale
    for part in range(parts):
        short_ref[:, part * LANES : (part + 1) * LANES] = (
            sums_ref[part, 8 : 8 + short_ref.shape[0]] * short_scale
        )


def params(mib):
    return pltpu.CompilerParams(vmem_limit_bytes=mib * MIB)


def cost(flops, moved):
    return pl.CostEstimate(flops=flops, bytes_accessed=moved, transcendentals=0)


def columns(rows):
    return pl.BlockSpec((rows, TILE), lambda step: (0, step))


def whole(array):
    return pl.BlockSpec(array.shape, lambda step: (0,) * array.ndim)


def body(queries, products, packed_grad, packed_target, short_filter, medium_filter):
    query, product = queries[0], products[0]
    rows, channels = product.shape
    group_count = medium_filter.shape[1]
    per_group = channels // group_count
    short_count = short_filter.shape[0]
    shards, copies = lax.axis_size("seq"), lax.axis_size("dp")
    capacity = 2 * rows // shards
    slots = shards * capacity
    width = channels + rows
    steps = channels // TILE
    table = wave_table(rows)
    fh, fl = halves(table)
    ih, il = halves(table.T / rows)
    ch, cl = halves(table[:, :rows] / rows)
    f32, bf16 = jnp.float32, jnp.bfloat16

    with jax.named_scope("pack"):
        send = pl.pallas_call(
            lambda *refs: pack_kernel(capacity, *refs),
            out_shape=jax.ShapeDtypeStruct((slots, width), bf16),
            compiler_params=params(24),
            cost_estimate=cost(2 * slots * rows * width, 8 * MIB // 2),
        )(packed_target, packed_grad[0])
    with jax.named_scope("route"):
        recv = lax.all_to_all(
            send.reshape(shards, capacity, width), "seq", split_axis=0, concat_axis=0, tiled=True
        ).reshape(slots, width)
    with jax.named_scope("halo"):
        onward = [(index, index + 1) for index in range(shards - 1)]
        prev = lax.ppermute(product, "seq", onward)
        tail = lax.ppermute(query[rows - 16 :], "seq", onward)
    with jax.named_scope("early"):
        smoothed, hidden, spec = pl.pallas_call(
            lambda *refs: early_kernel(per_group, *refs),
            grid=(steps,),
            in_specs=[
                columns(rows),
                columns(16),
                columns(rows),
                columns(rows),
                columns(short_count),
                whole(medium_filter),
                whole(fh),
                whole(fl),
                whole(ih),
                whole(il),
            ],
            out_specs=[columns(rows), columns(rows), columns(2 * rows)],
            out_shape=[
                jax.ShapeDtypeStruct((rows, channels), f32),
                jax.ShapeDtypeStruct((rows, channels), f32),
                jax.ShapeDtypeStruct((2 * rows, channels), f32),
            ],
            compiler_params=params(32),
            cost_estimate=cost(16 * rows * 2 * rows * channels, 12 * MIB),
        )(query, tail, product, prev, short_filter, medium_filter, fh, fl, ih, il)
    with jax.named_scope("grads"):
        hgrad, sums = pl.pallas_call(
            lambda *refs: grad_kernel(per_group, short_count, *refs),
            grid=(steps,),
            in_specs=[
                pl.BlockSpec((slots, rows), lambda step: (0, channels // rows)),
                columns(slots),
                columns(rows),
                columns(rows),
                columns(2 * rows),
                columns(rows),
                columns(16),
                whole(fh),
                whole(fl),
                whole(ch),
                whole(cl),
            ],
            out_specs=[
                columns(rows),
                pl.BlockSpec((TILE // LANES, BLOCK_ROWS, LANES), lambda step: (step, 0, 0)),
            ],
            out_shape=[
                jax.ShapeDtypeStruct((rows, channels), bf16),
                jax.ShapeDtypeStruct((channels // LANES, BLOCK_ROWS, LANES), f32),
            ],
            compiler_params=params(32),
            cost_estimate=cost(10 * rows * 2 * rows * channels, 12 * MIB),
        )(recv, recv, smoothed, hidden, spec, query, tail, fh, fl, ch, cl)
    with jax.named_scope("sums_seq"):
        mine = jnp.sum(lax.all_to_all(sums, "seq", 0, 0, tiled=True), axis=0)
    with jax.named_scope("sums_dp"):
        spread = jnp.broadcast_to(mine[None], (copies, BLOCK_ROWS, LANES))
        mine = jnp.sum(lax.all_to_all(spread, "dp", 0, 0, tiled=True), axis=0)
    with jax.named_scope("sums_all"):
        spread = jnp.broadcast_to(mine[None], (shards, BLOCK_ROWS, LANES))
        total = lax.all_to_all(spread, "seq", 0, 0, tiled=True)
    with jax.named_scope("later"):
        following = lax.ppermute(
            hgrad, "seq", [(index + 1, index) for index in range(shards - 1)]
        )
    with jax.named_scope("input_grad"):
        input_grad = pl.pallas_call(
            lambda *refs: input_kernel(per_group, *refs),
            grid=(steps,),
            in_specs=[columns(rows), columns(rows)]
            + [whole(medium_filter), whole(fh), whole(fl), whole(ih), whole(il)],
            out_specs=columns(rows),
            out_shape=jax.ShapeDtypeStruct((rows, channels), bf16),
            compiler_params=params(32),
            cost_estimate=cost(16 * rows * 2 * rows * channels, 4 * MIB),
        )(hgrad, following, medium_filter, fh, fl, ih, il)
    with jax.named_scope("finish"):
        positions = copies * shards * rows
        medium_scale = 1.0 / math.sqrt(positions * per_group)
        short_scale = 1.0 / math.sqrt(positions)
        medium_grad, short_grad = pl.pallas_call(
            lambda *refs: last_kernel(medium_scale, short_scale, *refs),
            out_shape=[
                jax.ShapeDtypeStruct((rows, group_count), f32),
                jax.ShapeDtypeStruct((short_count, channels), f32),
            ],
        )(total)
    return input_grad[None], medium_grad, short_grad


def solution(mesh):
    in_specs = (
        P("dp", "seq", None),
        P("dp", "seq", None),
        P("dp", "seq", None),
        P("dp", "seq"),
        P(),
        P(),
    )
    out_specs = (P("dp", "seq", None), P(), P())
    return jax.shard_map(body, mesh=mesh, in_specs=in_specs, out_specs=out_specs, check_vma=False)
```

```python
import math

import jax
import jax.numpy as jnp
import numpy as np
from jax import lax
from jax.experimental import pallas as pl
from jax.experimental.pallas import tpu as pltpu
from jax.sharding import PartitionSpec as P

TILE = 1024
LANES = 128
BLOCK_ROWS = 16
MIB = 1024 * 1024


def split(value):
    high = value.astype(jnp.bfloat16)
    low = (value - high.astype(jnp.float32)).astype(jnp.bfloat16)
    return high, low


def wave_table(rows):
    size = 2 * rows
    phase = (np.arange(size)[None, :] * (2 * np.arange(rows)[:, None] + 1)) % (2 * size)
    angle = phase * (math.pi / size)
    return np.concatenate([np.cos(angle), -np.sin(angle)], axis=0)


def halves(table):
    high = table.astype(jnp.bfloat16)
    low = (table - high.astype(np.float64)).astype(jnp.bfloat16)
    return jnp.asarray(np.concatenate([high, low], axis=0))


def mm(left, right):
    return jnp.dot(left, right, preferred_element_type=jnp.float32)


def forward(table, value):
    both = mm(table, value)
    half = both.shape[0] // 2
    return both[:half] + both[half:]


def backward(table, value):
    top, rest = split(value)
    return forward(table, top) + mm(table[: table.shape[0] // 2], rest)


def halved(spec):
    half = spec.shape[0] // 2
    return spec[:half], spec[half:]


def filter_spec(taps, table, per_group):
    tap_count, group_count = taps.shape
    channel = lax.broadcasted_iota(jnp.int32, (group_count, TILE), 1) + pl.program_id(0) * TILE
    group = lax.broadcasted_iota(jnp.int32, (group_count, TILE), 0)
    first = group * per_group
    expand = ((channel >= first) & (channel < first + per_group)).astype(jnp.bfloat16)
    wide = mm(taps, expand).astype(jnp.bfloat16)
    return forward(table[:, :tap_count], wide)


def delayed(query, tail, steps):
    moved = pltpu.roll(query, steps, 0)
    row = lax.broadcasted_iota(jnp.int32, query.shape, 0)
    for index in range(steps):
        source = tail.shape[0] - steps + index
        moved = jnp.where(row == index, tail[source : source + 1], moved)
    return moved


def smoothing(query, tail, short):
    moved = [query] + [delayed(query, tail, offset) for offset in range(1, short.shape[0])]
    return sum(short[offset : offset + 1] * value for offset, value in enumerate(moved)), moved


def pack_kernel(capacity, target_ref, grad_ref, out_ref, block, held, come, leave):
    rows, channels = grad_ref.shape
    slots = out_ref.shape[0]
    parts = channels // TILE
    arriving = []
    for index in range(parts):
        cut = pl.ds(index * TILE, TILE)
        arriving.append(
            pltpu.make_async_copy(grad_ref.at[:, cut], block.at[:, cut], come.at[index])
        )
        arriving[-1].start()

    def leaving(cut, index):
        return pltpu.make_async_copy(held.at[:, cut], out_ref.at[:, cut], leave.at[index])

    wide = jnp.broadcast_to(target_ref[...].astype(jnp.float32), (rows, rows))
    across = wide.astype(jnp.int32)
    down = wide.T.astype(jnp.int32)
    upper = lax.broadcasted_iota(jnp.int32, (rows, rows), 0)
    right = lax.broadcasted_iota(jnp.int32, (rows, rows), 1)
    owner = lax.div(across, rows)
    earlier = (owner == lax.div(down, rows)) & (upper < right)
    rank = jnp.sum(earlier.astype(jnp.float32), axis=0, keepdims=True).astype(jnp.int32)
    slot = owner[:1] * capacity + rank
    placing = (lax.broadcasted_iota(jnp.int32, (slots, rows), 0) == slot).astype(jnp.bfloat16)
    for index, copy in enumerate(arriving):
        cut = pl.ds(index * TILE, TILE)
        copy.wait()
        held[:, cut] = mm(placing, block[:, cut]).astype(jnp.bfloat16)
        leaving(cut, index).start()
    landing = (lax.rem(down, rows) == right).astype(jnp.bfloat16)
    held[:, channels:] = mm(placing, landing).astype(jnp.bfloat16)
    leaving(pl.ds(channels, rows), parts).start()
    for index in range(parts):
        leaving(pl.ds(index * TILE, TILE), index).wait()
    leaving(pl.ds(channels, rows), parts).wait()


def early_kernel(
    per_group,
    own_ref,
    prev_ref,
    taps_ref,
    ft_ref,
    it_ref,
    hidden_ref,
    spec_ref,
):
    spec = forward(ft_ref[...], jnp.concatenate([prev_ref[...], own_ref[...]], axis=0))
    spec_ref[...] = spec
    wave = filter_spec(taps_ref[...], ft_ref, per_group)
    sr, si = halved(spec)
    wr, wi = halved(wave)
    product = jnp.concatenate([sr * wr - si * wi, sr * wi + si * wr], axis=0)
    hidden_ref[...] = backward(it_ref[...], product)


def grad_kernel(
    per_group,
    land_ref,
    recv_ref,
    hidden_ref,
    spec_ref,
    query_ref,
    tail_ref,
    short_ref,
    ft_ref,
    ct_ref,
    hgrad_ref,
    sums_ref,
):
    rows = hgrad_ref.shape[0]
    groups = TILE // per_group
    routed = lax.dot_general(
        land_ref[...],
        recv_ref[...],
        (((0,), (0,)), ((), ())),
        preferred_element_type=jnp.float32,
    )
    query = query_ref[...].astype(jnp.float32)
    tail = tail_ref[...].astype(jnp.float32)
    smoothed, moved = smoothing(query, tail, short_ref[...].astype(jnp.float32))
    hgrad = (routed * smoothed).astype(jnp.bfloat16)
    hgrad_ref[...] = hgrad
    sgrad = routed * hidden_ref[...]
    terms = [jnp.sum(sgrad * value, axis=0, keepdims=True) for value in moved]
    terms.append(jnp.zeros((8 - len(moved), TILE), jnp.float32))
    short_terms = jnp.concatenate(terms, axis=0)
    gr, gi = halved(forward(ft_ref[:, rows:], hgrad))
    pr, pi = halved(spec_ref[...])
    cross = jnp.concatenate([gr * pr + gi * pi, gi * pr - gr * pi], axis=0)
    first = lax.broadcasted_iota(jnp.int32, (TILE, groups), 1) * per_group
    channel = lax.broadcasted_iota(jnp.int32, (TILE, groups), 0)
    member = ((channel >= first) & (channel < first + per_group)).astype(jnp.bfloat16)
    top, rest = split(cross)
    grouped = forward(jnp.concatenate([top, rest], axis=0), member)
    lagged = backward(ct_ref[...], grouped).T
    for part in range(TILE // LANES):
        sums_ref[part, :8] = lagged[8 * part : 8 * part + 8]
        sums_ref[part, 8:] = short_terms[:, part * LANES : (part + 1) * LANES]


def own_kernel(per_group, own_ref, taps_ref, ft_ref, it_ref, part_ref):
    rows = own_ref.shape[0]
    gr, gi = halved(forward(ft_ref[:, :rows], own_ref[...]))
    wr, wi = halved(filter_spec(taps_ref[...], ft_ref, per_group))
    product = jnp.concatenate([gr * wr + gi * wi, gi * wr - gr * wi], axis=0)
    part_ref[...] = backward(it_ref[...], product)


def input_kernel(per_group, part_ref, next_ref, taps_ref, ft_ref, it_ref, out_ref):
    rows = next_ref.shape[0]
    gr, gi = halved(forward(ft_ref[:, rows:], next_ref[...]))
    wr, wi = halved(filter_spec(taps_ref[...], ft_ref, per_group))
    product = jnp.concatenate([gr * wr + gi * wi, gi * wr - gr * wi], axis=0)
    out_ref[...] = (part_ref[...] + backward(it_ref[...], product)).astype(jnp.bfloat16)


def last_kernel(medium_scale, short_scale, sums_ref, medium_ref, short_ref):
    parts = sums_ref.shape[0]
    groups = medium_ref.shape[1]
    medium = sums_ref[:, :8, :].reshape(groups, LANES)
    medium_ref[...] = medium.T * medium_scale
    for part in range(parts):
        short_ref[:, part * LANES : (part + 1) * LANES] = (
            sums_ref[part, 8 : 8 + short_ref.shape[0]] * short_scale
        )


def params(mib):
    return pltpu.CompilerParams(vmem_limit_bytes=mib * MIB)


def cost(flops, moved):
    return pl.CostEstimate(flops=flops, bytes_accessed=moved, transcendentals=0)


def columns(rows):
    return pl.BlockSpec((rows, TILE), lambda step: (0, step))


def whole(array):
    return pl.BlockSpec(array.shape, lambda step: (0,) * array.ndim)


def body(queries, products, packed_grad, packed_target, short_filter, medium_filter):
    query, product = queries[0], products[0]
    rows, channels = product.shape
    group_count = medium_filter.shape[1]
    per_group = channels // group_count
    short_count = short_filter.shape[0]
    shards, copies = lax.axis_size("seq"), lax.axis_size("dp")
    capacity = 2 * rows // shards
    slots = shards * capacity
    width = channels + rows
    steps = channels // TILE
    table = wave_table(rows)
    forth = halves(table)
    first = halves(table.T[:rows] / rows)
    second = halves(table.T[rows:] / rows)
    f32, bf16 = jnp.float32, jnp.bfloat16

    with jax.named_scope("pack"):
        send = pl.pallas_call(
            lambda *refs: pack_kernel(capacity, *refs),
            in_specs=[
                pl.BlockSpec(memory_space=pltpu.VMEM),
                pl.BlockSpec(memory_space=pl.ANY),
            ],
            out_specs=pl.BlockSpec(memory_space=pl.ANY),
            scratch_shapes=[
                pltpu.VMEM((rows, channels), bf16),
                pltpu.VMEM((slots, width), bf16),
                pltpu.SemaphoreType.DMA((steps,)),
                pltpu.SemaphoreType.DMA((steps + 1,)),
            ],
            out_shape=jax.ShapeDtypeStruct((slots, width), bf16),
            compiler_params=params(56),
            cost_estimate=cost(2 * slots * rows * width, 8 * MIB // 2),
        )(packed_target, packed_grad[0])
    with jax.named_scope("route"):
        recv = lax.all_to_all(
            send.reshape(shards, capacity, width), "seq", split_axis=0, concat_axis=0, tiled=True
        ).reshape(slots, width)
    with jax.named_scope("halo"):
        onward = [(index, index + 1) for index in range(shards - 1)]
        prev = lax.ppermute(product, "seq", onward)
    with jax.named_scope("early"):
        hidden, spec = pl.pallas_call(
            lambda *refs: early_kernel(per_group, *refs),
            grid=(steps,),
            in_specs=[
                columns(rows),
                columns(rows),
                whole(medium_filter),
                whole(forth),
                whole(second),
            ],
            out_specs=[columns(rows), columns(2 * rows)],
            out_shape=[
                jax.ShapeDtypeStruct((rows, channels), f32),
                jax.ShapeDtypeStruct((2 * rows, channels), f32),
            ],
            compiler_params=params(56),
            cost_estimate=cost(10**14, 12 * MIB),
        )(product, prev, medium_filter, forth, second)
    with jax.named_scope("tail"):
        ending, hidden = lax.optimization_barrier((query, hidden))
        tail = lax.ppermute(ending[rows - 16 :], "seq", onward)
    with jax.named_scope("grads"):
        hgrad, sums = pl.pallas_call(
            lambda *refs: grad_kernel(per_group, *refs),
            grid=(steps,),
            in_specs=[
                pl.BlockSpec((slots, rows), lambda step: (0, channels // rows)),
                columns(slots),
                columns(rows),
                columns(2 * rows),
                columns(rows),
                columns(16),
                columns(short_count),
                whole(forth),
                whole(first),
            ],
            out_specs=[
                columns(rows),
                pl.BlockSpec((TILE // LANES, BLOCK_ROWS, LANES), lambda step: (step, 0, 0)),
            ],
            out_shape=[
                jax.ShapeDtypeStruct((rows, channels), bf16),
                jax.ShapeDtypeStruct((channels // LANES, BLOCK_ROWS, LANES), f32),
            ],
            compiler_params=params(56),
            cost_estimate=cost(10 * rows * 2 * rows * channels, 12 * MIB),
        )(recv, recv, hidden, spec, query, tail, short_filter, forth, first)
    with jax.named_scope("sums_seq"):
        mine = jnp.sum(lax.all_to_all(sums, "seq", 0, 0, tiled=True), axis=0)
    with jax.named_scope("own_rows"):
        part = pl.pallas_call(
            lambda *refs: own_kernel(per_group, *refs),
            grid=(steps,),
            in_specs=[columns(rows)] + [whole(medium_filter), whole(forth), whole(first)],
            out_specs=columns(rows),
            out_shape=jax.ShapeDtypeStruct((rows, channels), f32),
            compiler_params=params(56),
            cost_estimate=cost(16 * rows * 2 * rows * channels, 3 * MIB),
        )(hgrad, medium_filter, forth, first)
    with jax.named_scope("later"):
        part, leaving = lax.optimization_barrier((part, hgrad))
        following = lax.ppermute(
            leaving, "seq", [(index + 1, index) for index in range(shards - 1)]
        )
    with jax.named_scope("sums_dp"):
        spread = jnp.broadcast_to(mine[None], (copies, BLOCK_ROWS, LANES))
        mine = jnp.sum(lax.all_to_all(spread, "dp", 0, 0, tiled=True), axis=0)
    with jax.named_scope("input_grad"):
        input_grad = pl.pallas_call(
            lambda *refs: input_kernel(per_group, *refs),
            grid=(steps,),
            in_specs=[columns(rows), columns(rows)]
            + [whole(medium_filter), whole(forth), whole(first)],
            out_specs=columns(rows),
            out_shape=jax.ShapeDtypeStruct((rows, channels), bf16),
            compiler_params=params(56),
            cost_estimate=cost(16 * rows * 2 * rows * channels, 4 * MIB),
        )(part, following, medium_filter, forth, first)
    with jax.named_scope("sums_all"):
        spread = jnp.broadcast_to(mine[None], (shards, BLOCK_ROWS, LANES))
        total = lax.all_to_all(spread, "seq", 0, 0, tiled=True)
    with jax.named_scope("finish"):
        positions = copies * shards * rows
        medium_scale = 1.0 / math.sqrt(positions * per_group)
        short_scale = 1.0 / math.sqrt(positions)
        medium_grad, short_grad = pl.pallas_call(
            lambda *refs: last_kernel(medium_scale, short_scale, *refs),
            out_shape=[
                jax.ShapeDtypeStruct((rows, group_count), f32),
                jax.ShapeDtypeStruct((short_count, channels), f32),
            ],
            compiler_params=params(56),
        )(total)
    return input_grad[None], medium_grad, short_grad


def solution(mesh):
    in_specs = (
        P("dp", "seq", None),
        P("dp", "seq", None),
        P("dp", "seq", None),
        P("dp", "seq"),
        P(),
        P(),
    )
    out_specs = (P("dp", "seq", None), P(), P())
    return jax.shard_map(body, mesh=mesh, in_specs=in_specs, out_specs=out_specs, check_vma=False)
```

```python
import math

import jax
import jax.numpy as jnp
import numpy as np
from jax import lax
from jax.experimental import pallas as pl
from jax.experimental.pallas import tpu as pltpu
from jax.sharding import PartitionSpec as P

TILE = 1024
WIDE = 2048
LANES = 128
BLOCK_ROWS = 16
MIB = 1024 * 1024


def split(value):
    high = value.astype(jnp.bfloat16)
    low = (value - high.astype(jnp.float32)).astype(jnp.bfloat16)
    return high, low


def wave_table(rows):
    size = 2 * rows
    phase = (np.arange(size)[None, :] * (2 * np.arange(rows)[:, None] + 1)) % (2 * size)
    angle = phase * (math.pi / size)
    return np.concatenate([np.cos(angle), -np.sin(angle)], axis=0)


def halves(table):
    high = table.astype(jnp.bfloat16)
    low = (table - high.astype(np.float64)).astype(jnp.bfloat16)
    return jnp.asarray(np.concatenate([high, low], axis=0))


def beside(table, start, stop):
    half = table.shape[0] // 2
    return jnp.concatenate([table[:half, start:stop], table[half:, start:stop]], axis=1)


def mm(left, right):
    return jnp.dot(left, right, preferred_element_type=jnp.float32)


def forward(table, value):
    both = mm(table, value)
    half = both.shape[0] // 2
    return both[:half] + both[half:]


def narrow(table, value):
    return mm(table, jnp.concatenate([value, value], axis=0))


def backward(table, value):
    top, rest = split(value)
    return forward(table, top) + mm(table[: table.shape[0] // 2], rest)


def halved(spec):
    half = spec.shape[0] // 2
    return spec[:half], spec[half:]


def filter_spec(taps, table, per_group, tile):
    group_count = taps.shape[1]
    channel = lax.broadcasted_iota(jnp.int32, (group_count, tile), 1) + pl.program_id(0) * tile
    group = lax.broadcasted_iota(jnp.int32, (group_count, tile), 0)
    first = group * per_group
    expand = ((channel >= first) & (channel < first + per_group)).astype(jnp.bfloat16)
    wide = mm(taps, expand).astype(jnp.bfloat16)
    return narrow(table, wide)


def delayed(query, tail, steps):
    moved = pltpu.roll(query, steps, 0)
    row = lax.broadcasted_iota(jnp.int32, query.shape, 0)
    for index in range(steps):
        source = tail.shape[0] - steps + index
        moved = jnp.where(row == index, tail[source : source + 1], moved)
    return moved


def smoothing(query, tail, short):
    moved = [query] + [delayed(query, tail, offset) for offset in range(1, short.shape[0])]
    return sum(short[offset : offset + 1] * value for offset, value in enumerate(moved)), moved


def pack_kernel(capacity, target_ref, grad_ref, out_ref, block, held, come, leave):
    rows, channels = grad_ref.shape
    slots = out_ref.shape[0]
    parts = channels // TILE
    arriving = []
    for index in range(parts):
        cut = pl.ds(index * TILE, TILE)
        arriving.append(
            pltpu.make_async_copy(grad_ref.at[:, cut], block.at[:, cut], come.at[index])
        )
        arriving[-1].start()

    def leaving(cut, index):
        return pltpu.make_async_copy(held.at[:, cut], out_ref.at[:, cut], leave.at[index])

    wide = jnp.broadcast_to(target_ref[...].astype(jnp.float32), (rows, rows))
    across = wide.astype(jnp.int32)
    down = wide.T.astype(jnp.int32)
    upper = lax.broadcasted_iota(jnp.int32, (rows, rows), 0)
    right = lax.broadcasted_iota(jnp.int32, (rows, rows), 1)
    owner = lax.div(across, rows)
    earlier = (owner == lax.div(down, rows)) & (upper < right)
    rank = jnp.sum(earlier.astype(jnp.float32), axis=0, keepdims=True).astype(jnp.int32)
    slot = owner[:1] * capacity + rank
    placing = (lax.broadcasted_iota(jnp.int32, (slots, rows), 0) == slot).astype(jnp.bfloat16)
    for index, copy in enumerate(arriving):
        cut = pl.ds(index * TILE, TILE)
        copy.wait()
        held[:, cut] = mm(placing, block[:, cut]).astype(jnp.bfloat16)
        leaving(cut, index).start()
    landing = (lax.rem(down, rows) == right).astype(jnp.bfloat16)
    held[:, channels:] = mm(placing, landing).astype(jnp.bfloat16)
    leaving(pl.ds(channels, rows), parts).start()
    for index in range(parts):
        leaving(pl.ds(index * TILE, TILE), index).wait()
    leaving(pl.ds(channels, rows), parts).wait()


def early_kernel(
    per_group,
    own_ref,
    prev_ref,
    taps_ref,
    ft_ref,
    fn_ref,
    it_ref,
    hidden_ref,
    spec_ref,
):
    spec = forward(ft_ref[...], jnp.concatenate([prev_ref[...], own_ref[...]], axis=0))
    spec_ref[...] = spec
    wave = filter_spec(taps_ref[...], fn_ref[...], per_group, own_ref.shape[1])
    sr, si = halved(spec)
    wr, wi = halved(wave)
    product = jnp.concatenate([sr * wr - si * wi, sr * wi + si * wr], axis=0)
    hidden_ref[...] = backward(it_ref[...], product)


def grad_kernel(
    per_group,
    land_ref,
    recv_ref,
    hidden_ref,
    spec_ref,
    query_ref,
    tail_ref,
    short_ref,
    fn_ref,
    ct_ref,
    hgrad_ref,
    sums_ref,
):
    tile = hgrad_ref.shape[1]
    groups = tile // per_group
    routed = lax.dot_general(
        land_ref[...],
        recv_ref[...],
        (((0,), (0,)), ((), ())),
        preferred_element_type=jnp.float32,
    )
    query = query_ref[...].astype(jnp.float32)
    tail = tail_ref[...].astype(jnp.float32)
    smoothed, moved = smoothing(query, tail, short_ref[...].astype(jnp.float32))
    hgrad = (routed * smoothed).astype(jnp.bfloat16)
    hgrad_ref[...] = hgrad
    sgrad = routed * hidden_ref[...]
    terms = [jnp.sum(sgrad * value, axis=0, keepdims=True) for value in moved]
    terms.append(jnp.zeros((8 - len(moved), tile), jnp.float32))
    short_terms = jnp.concatenate(terms, axis=0)
    gr, gi = halved(narrow(fn_ref[...], hgrad))
    pr, pi = halved(spec_ref[...])
    cross = jnp.concatenate([gr * pr + gi * pi, gi * pr - gr * pi], axis=0)
    first = lax.broadcasted_iota(jnp.int32, (tile, groups), 1) * per_group
    channel = lax.broadcasted_iota(jnp.int32, (tile, groups), 0)
    member = ((channel >= first) & (channel < first + per_group)).astype(jnp.bfloat16)
    top, rest = split(cross)
    grouped = forward(jnp.concatenate([top, rest], axis=0), member)
    lagged = backward(ct_ref[...], grouped).T
    for part in range(tile // LANES):
        sums_ref[part, :8] = lagged[8 * part : 8 * part + 8]
        sums_ref[part, 8:] = short_terms[:, part * LANES : (part + 1) * LANES]


def own_kernel(per_group, own_ref, taps_ref, fn_ref, it_ref, part_ref):
    gr, gi = halved(narrow(fn_ref[...], own_ref[...]))
    wr, wi = halved(filter_spec(taps_ref[...], fn_ref[...], per_group, own_ref.shape[1]))
    product = jnp.concatenate([gr * wr + gi * wi, gi * wr - gr * wi], axis=0)
    part_ref[...] = backward(it_ref[...], product)


def input_kernel(per_group, part_ref, next_ref, taps_ref, fn_ref, gn_ref, it_ref, out_ref):
    gr, gi = halved(narrow(gn_ref[...], next_ref[...]))
    wr, wi = halved(filter_spec(taps_ref[...], fn_ref[...], per_group, next_ref.shape[1]))
    product = jnp.concatenate([gr * wr + gi * wi, gi * wr - gr * wi], axis=0)
    out_ref[...] = (part_ref[...] + backward(it_ref[...], product)).astype(jnp.bfloat16)


def last_kernel(medium_scale, short_scale, sums_ref, medium_ref, short_ref):
    parts = sums_ref.shape[0]
    groups = medium_ref.shape[1]
    medium = sums_ref[:, :8, :].reshape(groups, LANES)
    medium_ref[...] = medium.T * medium_scale
    for part in range(parts):
        short_ref[:, part * LANES : (part + 1) * LANES] = (
            sums_ref[part, 8 : 8 + short_ref.shape[0]] * short_scale
        )


def params(mib):
    return pltpu.CompilerParams(vmem_limit_bytes=mib * MIB)


def cost(flops, moved):
    return pl.CostEstimate(flops=flops, bytes_accessed=moved, transcendentals=0)


def columns(rows, tile=WIDE):
    return pl.BlockSpec((rows, tile), lambda step: (0, step))


def whole(array):
    return pl.BlockSpec(array.shape, lambda step: (0,) * array.ndim)


def body(queries, products, packed_grad, packed_target, short_filter, medium_filter):
    query, product = queries[0], products[0]
    rows, channels = product.shape
    group_count = medium_filter.shape[1]
    per_group = channels // group_count
    short_count = short_filter.shape[0]
    shards, copies = lax.axis_size("seq"), lax.axis_size("dp")
    capacity = 2 * rows // shards
    slots = shards * capacity
    width = channels + rows
    chunks = channels // TILE
    steps = channels // WIDE
    table = wave_table(rows)
    forth = halves(table)
    lower = beside(forth, 0, rows)
    upper = beside(forth, rows, 2 * rows)
    first = halves(table.T[:rows] / rows)
    second = halves(table.T[rows:] / rows)
    f32, bf16 = jnp.float32, jnp.bfloat16

    with jax.named_scope("pack"):
        send = pl.pallas_call(
            lambda *refs: pack_kernel(capacity, *refs),
            in_specs=[
                pl.BlockSpec(memory_space=pltpu.VMEM),
                pl.BlockSpec(memory_space=pl.ANY),
            ],
            out_specs=pl.BlockSpec(memory_space=pl.ANY),
            scratch_shapes=[
                pltpu.VMEM((rows, channels), bf16),
                pltpu.VMEM((slots, width), bf16),
                pltpu.SemaphoreType.DMA((chunks,)),
                pltpu.SemaphoreType.DMA((chunks + 1,)),
            ],
            out_shape=jax.ShapeDtypeStruct((slots, width), bf16),
            compiler_params=params(60),
            cost_estimate=cost(2 * slots * rows * width, 8 * MIB // 2),
        )(packed_target, packed_grad[0])
    with jax.named_scope("route"):
        recv = lax.all_to_all(
            send.reshape(shards, capacity, width), "seq", split_axis=0, concat_axis=0, tiled=True
        ).reshape(slots, width)
    with jax.named_scope("halo"):
        onward = [(index, index + 1) for index in range(shards - 1)]
        prev = lax.ppermute(product, "seq", onward)
    with jax.named_scope("early"):
        hidden, spec = pl.pallas_call(
            lambda *refs: early_kernel(per_group, *refs),
            grid=(steps,),
            in_specs=[
                columns(rows),
                columns(rows),
                whole(medium_filter),
                whole(forth),
                whole(lower),
                whole(second),
            ],
            out_specs=[columns(rows), columns(2 * rows)],
            out_shape=[
                jax.ShapeDtypeStruct((rows, channels), f32),
                jax.ShapeDtypeStruct((2 * rows, channels), f32),
            ],
            compiler_params=params(60),
            cost_estimate=cost(10**14, 12 * MIB),
        )(product, prev, medium_filter, forth, lower, second)
    with jax.named_scope("tail"):
        ending, hidden = lax.optimization_barrier((query, hidden))
        tail = lax.ppermute(ending[rows - 16 :], "seq", onward)
    with jax.named_scope("grads"):
        hgrad, sums = pl.pallas_call(
            lambda *refs: grad_kernel(per_group, *refs),
            grid=(steps,),
            in_specs=[
                pl.BlockSpec((slots, rows), lambda step: (0, channels // rows)),
                columns(slots),
                columns(rows),
                columns(2 * rows),
                columns(rows),
                columns(16),
                columns(short_count),
                whole(upper),
                whole(first),
            ],
            out_specs=[
                columns(rows),
                pl.BlockSpec((WIDE // LANES, BLOCK_ROWS, LANES), lambda step: (step, 0, 0)),
            ],
            out_shape=[
                jax.ShapeDtypeStruct((rows, channels), bf16),
                jax.ShapeDtypeStruct((channels // LANES, BLOCK_ROWS, LANES), f32),
            ],
            compiler_params=params(60),
            cost_estimate=cost(10 * rows * 2 * rows * channels, 12 * MIB),
        )(recv, recv, hidden, spec, query, tail, short_filter, upper, first)
    with jax.named_scope("sums_seq"):
        mine = jnp.sum(lax.all_to_all(sums, "seq", 0, 0, tiled=True), axis=0)
    with jax.named_scope("own_rows"):
        part = pl.pallas_call(
            lambda *refs: own_kernel(per_group, *refs),
            grid=(steps,),
            in_specs=[columns(rows)] + [whole(medium_filter), whole(lower), whole(first)],
            out_specs=columns(rows),
            out_shape=jax.ShapeDtypeStruct((rows, channels), f32),
            compiler_params=params(60),
            cost_estimate=cost(16 * rows * 2 * rows * channels, 3 * MIB),
        )(hgrad, medium_filter, lower, first)
    with jax.named_scope("later"):
        part, leaving = lax.optimization_barrier((part, hgrad))
        following = lax.ppermute(
            leaving, "seq", [(index + 1, index) for index in range(shards - 1)]
        )
    with jax.named_scope("sums_dp"):
        spread = jnp.broadcast_to(mine[None], (copies, BLOCK_ROWS, LANES))
        mine = jnp.sum(lax.all_to_all(spread, "dp", 0, 0, tiled=True), axis=0)
    with jax.named_scope("input_grad"):
        input_grad = pl.pallas_call(
            lambda *refs: input_kernel(per_group, *refs),
            grid=(steps,),
            in_specs=[columns(rows), columns(rows)]
            + [whole(medium_filter), whole(lower), whole(upper), whole(first)],
            out_specs=columns(rows),
            out_shape=jax.ShapeDtypeStruct((rows, channels), bf16),
            compiler_params=params(60),
            cost_estimate=cost(16 * rows * 2 * rows * channels, 4 * MIB),
        )(part, following, medium_filter, lower, upper, first)
    with jax.named_scope("sums_all"):
        spread = jnp.broadcast_to(mine[None], (shards, BLOCK_ROWS, LANES))
        total = lax.all_to_all(spread, "seq", 0, 0, tiled=True)
    with jax.named_scope("finish"):
        positions = copies * shards * rows
        medium_scale = 1.0 / math.sqrt(positions * per_group)
        short_scale = 1.0 / math.sqrt(positions)
        medium_grad, short_grad = pl.pallas_call(
            lambda *refs: last_kernel(medium_scale, short_scale, *refs),
            out_shape=[
                jax.ShapeDtypeStruct((rows, group_count), f32),
                jax.ShapeDtypeStruct((short_count, channels), f32),
            ],
            compiler_params=params(8),
        )(total)
    return input_grad[None], medium_grad, short_grad


def solution(mesh):
    in_specs = (
        P("dp", "seq", None),
        P("dp", "seq", None),
        P("dp", "seq", None),
        P("dp", "seq"),
        P(),
        P(),
    )
    out_specs = (P("dp", "seq", None), P(), P())
    return jax.shard_map(body, mesh=mesh, in_specs=in_specs, out_specs=out_specs, check_vma=False)
```

```python
import math

import jax
import jax.numpy as jnp
import numpy as np
from jax import lax
from jax.experimental import pallas as pl
from jax.experimental.pallas import tpu as pltpu
from jax.sharding import PartitionSpec as P

TILE = 1024
WIDE = 2048
LANES = 128
BLOCK_ROWS = 16
MIB = 1024 * 1024


def split(value):
    high = value.astype(jnp.bfloat16)
    low = (value - high.astype(jnp.float32)).astype(jnp.bfloat16)
    return high, low


def wave_table(rows):
    size = 2 * rows
    phase = (np.arange(size)[None, :] * (2 * np.arange(rows)[:, None] + 1)) % (2 * size)
    angle = phase * (math.pi / size)
    return np.concatenate([np.cos(angle), -np.sin(angle)], axis=0)


def halves(table):
    high = table.astype(jnp.bfloat16)
    low = (table - high.astype(np.float64)).astype(jnp.bfloat16)
    return jnp.asarray(np.concatenate([high, low], axis=0))


def beside(table, start, stop):
    half = table.shape[0] // 2
    return jnp.concatenate([table[:half, start:stop], table[half:, start:stop]], axis=1)


def mm(left, right):
    return jnp.dot(left, right, preferred_element_type=jnp.float32)


def forward(table, value):
    both = mm(table, value)
    half = both.shape[0] // 2
    return both[:half] + both[half:]


def narrow(table, value):
    return mm(table, jnp.concatenate([value, value], axis=0))


def backward(table, value):
    top, rest = split(value)
    return forward(table, top) + mm(table[: table.shape[0] // 2], rest)


def halved(spec):
    half = spec.shape[0] // 2
    return spec[:half], spec[half:]


def filter_spec(taps, table, per_group, tile):
    group_count = taps.shape[1]
    channel = lax.broadcasted_iota(jnp.int32, (group_count, tile), 1) + pl.program_id(0) * tile
    group = lax.broadcasted_iota(jnp.int32, (group_count, tile), 0)
    first = group * per_group
    expand = ((channel >= first) & (channel < first + per_group)).astype(jnp.bfloat16)
    wide = mm(taps, expand).astype(jnp.bfloat16)
    return narrow(table, wide)


def delayed(query, tail, steps):
    moved = pltpu.roll(query, steps, 0)
    row = lax.broadcasted_iota(jnp.int32, query.shape, 0)
    for index in range(steps):
        source = tail.shape[0] - steps + index
        moved = jnp.where(row == index, tail[source : source + 1], moved)
    return moved


def smoothing(query, tail, short):
    moved = [query] + [delayed(query, tail, offset) for offset in range(1, short.shape[0])]
    return sum(short[offset : offset + 1] * value for offset, value in enumerate(moved)), moved


def pack_kernel(capacity, target_ref, grad_ref, out_ref, block, held, come, leave):
    rows, channels = grad_ref.shape
    slots = out_ref.shape[0]
    parts = channels // TILE
    arriving = []
    for index in range(parts):
        cut = pl.ds(index * TILE, TILE)
        arriving.append(
            pltpu.make_async_copy(grad_ref.at[:, cut], block.at[:, cut], come.at[index])
        )
        arriving[-1].start()

    def leaving(cut, index):
        return pltpu.make_async_copy(held.at[:, cut], out_ref.at[:, cut], leave.at[index])

    wide = jnp.broadcast_to(target_ref[...].astype(jnp.float32), (rows, rows))
    across = wide.astype(jnp.int32)
    down = wide.T.astype(jnp.int32)
    upper = lax.broadcasted_iota(jnp.int32, (rows, rows), 0)
    right = lax.broadcasted_iota(jnp.int32, (rows, rows), 1)
    owner = lax.div(across, rows)
    earlier = (owner == lax.div(down, rows)) & (upper < right)
    rank = jnp.sum(earlier.astype(jnp.float32), axis=0, keepdims=True).astype(jnp.int32)
    slot = owner[:1] * capacity + rank
    placing = (lax.broadcasted_iota(jnp.int32, (slots, rows), 0) == slot).astype(jnp.bfloat16)
    for index, copy in enumerate(arriving):
        cut = pl.ds(index * TILE, TILE)
        copy.wait()
        held[:, cut] = mm(placing, block[:, cut]).astype(jnp.bfloat16)
        leaving(cut, index).start()
    landing = (lax.rem(down, rows) == right).astype(jnp.bfloat16)
    held[:, channels:] = mm(placing, landing).astype(jnp.bfloat16)
    leaving(pl.ds(channels, rows), parts).start()
    for index in range(parts):
        leaving(pl.ds(index * TILE, TILE), index).wait()
    leaving(pl.ds(channels, rows), parts).wait()


def early_kernel(
    per_group,
    own_ref,
    prev_ref,
    taps_ref,
    ft_ref,
    fn_ref,
    it_ref,
    hidden_ref,
    spec_ref,
):
    spec = forward(ft_ref[...], jnp.concatenate([prev_ref[...], own_ref[...]], axis=0))
    spec_ref[...] = spec
    wave = filter_spec(taps_ref[...], fn_ref[...], per_group, own_ref.shape[1])
    sr, si = halved(spec)
    wr, wi = halved(wave)
    product = jnp.concatenate([sr * wr - si * wi, sr * wi + si * wr], axis=0)
    hidden_ref[...] = backward(it_ref[...], product)


def grad_kernel(
    per_group,
    land_ref,
    recv_ref,
    hidden_ref,
    spec_ref,
    query_ref,
    tail_ref,
    short_ref,
    fn_ref,
    ct_ref,
    hgrad_ref,
    sums_ref,
):
    tile = hgrad_ref.shape[1]
    groups = tile // per_group
    routed = lax.dot_general(
        land_ref[...],
        recv_ref[...],
        (((0,), (0,)), ((), ())),
        preferred_element_type=jnp.float32,
    )
    query = query_ref[...].astype(jnp.float32)
    tail = tail_ref[...].astype(jnp.float32)
    smoothed, moved = smoothing(query, tail, short_ref[...].astype(jnp.float32))
    hgrad = (routed * smoothed).astype(jnp.bfloat16)
    hgrad_ref[...] = hgrad
    sgrad = routed * hidden_ref[...]
    terms = [jnp.sum(sgrad * value, axis=0, keepdims=True) for value in moved]
    terms.append(jnp.zeros((8 - len(moved), tile), jnp.float32))
    short_terms = jnp.concatenate(terms, axis=0)
    gr, gi = halved(narrow(fn_ref[...], hgrad))
    pr, pi = halved(spec_ref[...])
    cross = jnp.concatenate([gr * pr + gi * pi, gi * pr - gr * pi], axis=0)
    first = lax.broadcasted_iota(jnp.int32, (tile, groups), 1) * per_group
    channel = lax.broadcasted_iota(jnp.int32, (tile, groups), 0)
    member = ((channel >= first) & (channel < first + per_group)).astype(jnp.bfloat16)
    top, rest = split(cross)
    grouped = forward(jnp.concatenate([top, rest], axis=0), member)
    lagged = backward(ct_ref[...], grouped).T
    for part in range(tile // LANES):
        sums_ref[part, :8] = lagged[8 * part : 8 * part + 8]
        sums_ref[part, 8:] = short_terms[:, part * LANES : (part + 1) * LANES]


def own_kernel(per_group, own_ref, taps_ref, fn_ref, it_ref, part_ref):
    gr, gi = halved(narrow(fn_ref[...], own_ref[...]))
    wr, wi = halved(filter_spec(taps_ref[...], fn_ref[...], per_group, own_ref.shape[1]))
    product = jnp.concatenate([gr * wr + gi * wi, gi * wr - gr * wi], axis=0)
    part_ref[...] = backward(it_ref[...], product)


def input_kernel(per_group, part_ref, next_ref, taps_ref, fn_ref, gn_ref, it_ref, out_ref):
    gr, gi = halved(narrow(gn_ref[...], next_ref[...]))
    wr, wi = halved(filter_spec(taps_ref[...], fn_ref[...], per_group, next_ref.shape[1]))
    product = jnp.concatenate([gr * wr + gi * wi, gi * wr - gr * wi], axis=0)
    out_ref[...] = (part_ref[...] + backward(it_ref[...], product)).astype(jnp.bfloat16)


def last_kernel(medium_scale, short_scale, sums_ref, medium_ref, short_ref):
    parts = sums_ref.shape[0]
    groups = medium_ref.shape[1]
    medium = sums_ref[:, :8, :].reshape(groups, LANES)
    medium_ref[...] = medium.T * medium_scale
    for part in range(parts):
        short_ref[:, part * LANES : (part + 1) * LANES] = (
            sums_ref[part, 8 : 8 + short_ref.shape[0]] * short_scale
        )


def params(mib):
    return pltpu.CompilerParams(vmem_limit_bytes=mib * MIB)


def cost(flops, moved):
    return pl.CostEstimate(flops=flops, bytes_accessed=moved, transcendentals=0)


def columns(rows, tile=WIDE):
    return pl.BlockSpec((rows, tile), lambda step: (0, step))


def whole(array):
    return pl.BlockSpec(array.shape, lambda step: (0,) * array.ndim)


def body(queries, products, packed_grad, packed_target, short_filter, medium_filter):
    query, product = queries[0], products[0]
    rows, channels = product.shape
    group_count = medium_filter.shape[1]
    per_group = channels // group_count
    short_count = short_filter.shape[0]
    shards, copies = lax.axis_size("seq"), lax.axis_size("dp")
    capacity = 2 * rows // shards
    slots = shards * capacity
    width = channels + rows
    chunks = channels // TILE
    steps = channels // WIDE
    table = wave_table(rows)
    forth = halves(table)
    lower = beside(forth, 0, rows)
    upper = beside(forth, rows, 2 * rows)
    first = halves(table.T[:rows] / rows)
    second = halves(table.T[rows:] / rows)
    f32, bf16 = jnp.float32, jnp.bfloat16

    with jax.named_scope("pack"):
        send = pl.pallas_call(
            lambda *refs: pack_kernel(capacity, *refs),
            in_specs=[
                pl.BlockSpec(memory_space=pltpu.VMEM),
                pl.BlockSpec(memory_space=pl.ANY),
            ],
            out_specs=pl.BlockSpec(memory_space=pl.ANY),
            scratch_shapes=[
                pltpu.VMEM((rows, channels), bf16),
                pltpu.VMEM((slots, width), bf16),
                pltpu.SemaphoreType.DMA((chunks,)),
                pltpu.SemaphoreType.DMA((chunks + 1,)),
            ],
            out_shape=jax.ShapeDtypeStruct((slots, width), bf16),
            compiler_params=params(60),
            cost_estimate=cost(2 * slots * rows * width, 8 * MIB // 2),
        )(packed_target, packed_grad[0])
    with jax.named_scope("route"):
        recv = lax.all_to_all(
            send.reshape(shards, capacity, width), "seq", split_axis=0, concat_axis=0, tiled=True
        ).reshape(slots, width)
    with jax.named_scope("halo"):
        onward = [(index, index + 1) for index in range(shards - 1)]
        prev = lax.ppermute(product, "seq", onward)
    with jax.named_scope("early"):
        hidden, spec = pl.pallas_call(
            lambda *refs: early_kernel(per_group, *refs),
            grid=(steps,),
            in_specs=[
                columns(rows),
                columns(rows),
                whole(medium_filter),
                whole(forth),
                whole(lower),
                whole(second),
            ],
            out_specs=[columns(rows), columns(2 * rows)],
            out_shape=[
                jax.ShapeDtypeStruct((rows, channels), f32),
                jax.ShapeDtypeStruct((2 * rows, channels), f32),
            ],
            compiler_params=params(60),
            cost_estimate=cost(10**14, 12 * MIB),
        )(product, prev, medium_filter, forth, lower, second)
    with jax.named_scope("tail"):
        ending, hidden = lax.optimization_barrier((query, hidden))
        tail = lax.ppermute(ending[rows - short_count + 1 :], "seq", onward)
    with jax.named_scope("grads"):
        hgrad, sums = pl.pallas_call(
            lambda *refs: grad_kernel(per_group, *refs),
            grid=(steps,),
            in_specs=[
                pl.BlockSpec((slots, rows), lambda step: (0, channels // rows)),
                columns(slots),
                columns(rows),
                columns(2 * rows),
                columns(rows),
                columns(short_count - 1),
                columns(short_count),
                whole(upper),
                whole(first),
            ],
            out_specs=[
                columns(rows),
                pl.BlockSpec((WIDE // LANES, BLOCK_ROWS, LANES), lambda step: (step, 0, 0)),
            ],
            out_shape=[
                jax.ShapeDtypeStruct((rows, channels), bf16),
                jax.ShapeDtypeStruct((channels // LANES, BLOCK_ROWS, LANES), f32),
            ],
            compiler_params=params(60),
            cost_estimate=cost(10 * rows * 2 * rows * channels, 12 * MIB),
        )(recv, recv, hidden, spec, query, tail, short_filter, upper, first)
    with jax.named_scope("sums_seq"):
        mine = jnp.sum(lax.all_to_all(sums, "seq", 0, 0, tiled=True), axis=0)
    with jax.named_scope("own_rows"):
        part = pl.pallas_call(
            lambda *refs: own_kernel(per_group, *refs),
            grid=(steps,),
            in_specs=[columns(rows)] + [whole(medium_filter), whole(lower), whole(first)],
            out_specs=columns(rows),
            out_shape=jax.ShapeDtypeStruct((rows, channels), f32),
            compiler_params=params(60),
            cost_estimate=cost(16 * rows * 2 * rows * channels, 3 * MIB),
        )(hgrad, medium_filter, lower, first)
    with jax.named_scope("later"):
        part, leaving = lax.optimization_barrier((part, hgrad))
        following = lax.ppermute(
            leaving, "seq", [(index + 1, index) for index in range(shards - 1)]
        )
    with jax.named_scope("sums_dp"):
        spread = jnp.broadcast_to(mine[None], (copies, BLOCK_ROWS, LANES))
        mine = jnp.sum(lax.all_to_all(spread, "dp", 0, 0, tiled=True), axis=0)
    with jax.named_scope("input_grad"):
        input_grad = pl.pallas_call(
            lambda *refs: input_kernel(per_group, *refs),
            grid=(steps,),
            in_specs=[columns(rows), columns(rows)]
            + [whole(medium_filter), whole(lower), whole(upper), whole(first)],
            out_specs=columns(rows),
            out_shape=jax.ShapeDtypeStruct((rows, channels), bf16),
            compiler_params=params(60),
            cost_estimate=cost(16 * rows * 2 * rows * channels, 4 * MIB),
        )(part, following, medium_filter, lower, upper, first)
    with jax.named_scope("sums_all"):
        spread = jnp.broadcast_to(mine[None], (shards, BLOCK_ROWS, LANES))
        total = lax.all_to_all(spread, "seq", 0, 0, tiled=True)
    with jax.named_scope("finish"):
        positions = copies * shards * rows
        medium_scale = 1.0 / math.sqrt(positions * per_group)
        short_scale = 1.0 / math.sqrt(positions)
        medium_grad, short_grad = pl.pallas_call(
            lambda *refs: last_kernel(medium_scale, short_scale, *refs),
            out_shape=[
                jax.ShapeDtypeStruct((rows, group_count), f32),
                jax.ShapeDtypeStruct((short_count, channels), f32),
            ],
            compiler_params=params(8),
        )(total)
    return input_grad[None], medium_grad, short_grad


def solution(mesh):
    in_specs = (
        P("dp", "seq", None),
        P("dp", "seq", None),
        P("dp", "seq", None),
        P("dp", "seq"),
        P(),
        P(),
    )
    out_specs = (P("dp", "seq", None), P(), P())
    return jax.shard_map(body, mesh=mesh, in_specs=in_specs, out_specs=out_specs, check_vma=False)
```

```python
import math

import jax
import jax.numpy as jnp
import numpy as np
from jax import lax
from jax.experimental import pallas as pl
from jax.experimental.pallas import tpu as pltpu
from jax.sharding import PartitionSpec as P

TILE = 1024
WIDE = 2048
LANES = 128
BLOCK_ROWS = 16
MIB = 1024 * 1024


def split(value):
    high = value.astype(jnp.bfloat16)
    low = (value - high.astype(jnp.float32)).astype(jnp.bfloat16)
    return high, low


def wave_table(rows):
    size = 2 * rows
    phase = (np.arange(size)[None, :] * (2 * np.arange(rows)[:, None] + 1)) % (2 * size)
    angle = phase * (math.pi / size)
    return np.concatenate([np.cos(angle), -np.sin(angle)], axis=0)


def halves(table):
    high = table.astype(jnp.bfloat16)
    low = (table - high.astype(np.float64)).astype(jnp.bfloat16)
    return jnp.asarray(np.concatenate([high, low], axis=0))


def beside(table, start, stop):
    half = table.shape[0] // 2
    return jnp.concatenate([table[:half, start:stop], table[half:, start:stop]], axis=1)


def mm(left, right):
    return jnp.dot(left, right, preferred_element_type=jnp.float32)


def forward(table, value):
    both = mm(table, value)
    half = both.shape[0] // 2
    return both[:half] + both[half:]


def narrow(table, value):
    return mm(table, jnp.concatenate([value, value], axis=0))


def backward(table, value):
    top, rest = split(value)
    return forward(table, top) + mm(table[: table.shape[0] // 2], rest)


def halved(spec):
    half = spec.shape[0] // 2
    return spec[:half], spec[half:]


def filter_spec(taps, table, per_group, tile):
    group_count = taps.shape[1]
    channel = lax.broadcasted_iota(jnp.int32, (group_count, tile), 1) + pl.program_id(0) * tile
    group = lax.broadcasted_iota(jnp.int32, (group_count, tile), 0)
    first = group * per_group
    expand = ((channel >= first) & (channel < first + per_group)).astype(jnp.bfloat16)
    wide = mm(taps, expand).astype(jnp.bfloat16)
    return narrow(table, wide)


def delayed(query, tail, steps):
    moved = pltpu.roll(query, steps, 0)
    row = lax.broadcasted_iota(jnp.int32, query.shape, 0)
    for index in range(steps):
        source = tail.shape[0] - steps + index
        moved = jnp.where(row == index, tail[source : source + 1], moved)
    return moved


def smoothing(query, tail, short):
    moved = [query] + [delayed(query, tail, offset) for offset in range(1, short.shape[0])]
    return sum(short[offset : offset + 1] * value for offset, value in enumerate(moved)), moved


def pack_kernel(capacity, target_ref, grad_ref, out_ref, block, held, come, leave):
    rows, channels = grad_ref.shape
    slots = out_ref.shape[0]
    parts = channels // TILE
    arriving = []
    for index in range(parts):
        cut = pl.ds(index * TILE, TILE)
        arriving.append(
            pltpu.make_async_copy(grad_ref.at[:, cut], block.at[:, cut], come.at[index])
        )
        arriving[-1].start()

    def leaving(cut, index):
        return pltpu.make_async_copy(held.at[:, cut], out_ref.at[:, cut], leave.at[index])

    wide = jnp.broadcast_to(target_ref[...].astype(jnp.float32), (rows, rows))
    across = wide.astype(jnp.int32)
    down = wide.T.astype(jnp.int32)
    upper = lax.broadcasted_iota(jnp.int32, (rows, rows), 0)
    right = lax.broadcasted_iota(jnp.int32, (rows, rows), 1)
    owner = lax.div(across, rows)
    earlier = (owner == lax.div(down, rows)) & (upper < right)
    rank = jnp.sum(earlier.astype(jnp.float32), axis=0, keepdims=True).astype(jnp.int32)
    slot = owner[:1] * capacity + rank
    placing = (lax.broadcasted_iota(jnp.int32, (slots, rows), 0) == slot).astype(jnp.bfloat16)
    for index, copy in enumerate(arriving):
        cut = pl.ds(index * TILE, TILE)
        copy.wait()
        held[:, cut] = mm(placing, block[:, cut]).astype(jnp.bfloat16)
        leaving(cut, index).start()
    landing = (lax.rem(down, rows) == right).astype(jnp.bfloat16)
    held[:, channels:] = mm(placing, landing).astype(jnp.bfloat16)
    leaving(pl.ds(channels, rows), parts).start()
    for index in range(parts):
        leaving(pl.ds(index * TILE, TILE), index).wait()
    leaving(pl.ds(channels, rows), parts).wait()


def early_kernel(
    per_group,
    own_ref,
    prev_ref,
    taps_ref,
    ft_ref,
    fn_ref,
    it_ref,
    hidden_ref,
    spec_ref,
):
    spec = forward(ft_ref[...], jnp.concatenate([prev_ref[...], own_ref[...]], axis=0))
    spec_ref[...] = spec.astype(jnp.bfloat16)
    wave = filter_spec(taps_ref[...], fn_ref[...], per_group, own_ref.shape[1])
    sr, si = halved(spec)
    wr, wi = halved(wave)
    product = jnp.concatenate([sr * wr - si * wi, sr * wi + si * wr], axis=0)
    hidden_ref[...] = backward(it_ref[...], product)


def grad_kernel(
    per_group,
    land_ref,
    recv_ref,
    hidden_ref,
    spec_ref,
    query_ref,
    tail_ref,
    short_ref,
    fn_ref,
    ct_ref,
    hgrad_ref,
    sums_ref,
):
    tile = hgrad_ref.shape[1]
    groups = tile // per_group
    routed = lax.dot_general(
        land_ref[...],
        recv_ref[...],
        (((0,), (0,)), ((), ())),
        preferred_element_type=jnp.float32,
    )
    query = query_ref[...].astype(jnp.float32)
    tail = tail_ref[...].astype(jnp.float32)
    smoothed, moved = smoothing(query, tail, short_ref[...].astype(jnp.float32))
    hgrad = (routed * smoothed).astype(jnp.bfloat16)
    hgrad_ref[...] = hgrad
    sgrad = routed * hidden_ref[...]
    terms = [jnp.sum(sgrad * value, axis=0, keepdims=True) for value in moved]
    terms.append(jnp.zeros((8 - len(moved), tile), jnp.float32))
    short_terms = jnp.concatenate(terms, axis=0)
    gr, gi = halved(narrow(fn_ref[...], hgrad))
    pr, pi = halved(spec_ref[...].astype(jnp.float32))
    cross = jnp.concatenate([gr * pr + gi * pi, gi * pr - gr * pi], axis=0)
    first = lax.broadcasted_iota(jnp.int32, (tile, groups), 1) * per_group
    channel = lax.broadcasted_iota(jnp.int32, (tile, groups), 0)
    member = ((channel >= first) & (channel < first + per_group)).astype(jnp.bfloat16)
    grouped = mm(cross.astype(jnp.bfloat16), member)
    lagged = backward(ct_ref[...], grouped).T
    for part in range(tile // LANES):
        sums_ref[part, :8] = lagged[8 * part : 8 * part + 8]
        sums_ref[part, 8:] = short_terms[:, part * LANES : (part + 1) * LANES]


def own_kernel(per_group, own_ref, taps_ref, fn_ref, it_ref, part_ref):
    gr, gi = halved(narrow(fn_ref[...], own_ref[...]))
    wr, wi = halved(filter_spec(taps_ref[...], fn_ref[...], per_group, own_ref.shape[1]))
    product = jnp.concatenate([gr * wr + gi * wi, gi * wr - gr * wi], axis=0)
    part_ref[...] = backward(it_ref[...], product)


def input_kernel(per_group, part_ref, next_ref, taps_ref, fn_ref, gn_ref, it_ref, out_ref):
    gr, gi = halved(narrow(gn_ref[...], next_ref[...]))
    wr, wi = halved(filter_spec(taps_ref[...], fn_ref[...], per_group, next_ref.shape[1]))
    product = jnp.concatenate([gr * wr + gi * wi, gi * wr - gr * wi], axis=0)
    out_ref[...] = (part_ref[...] + backward(it_ref[...], product)).astype(jnp.bfloat16)


def last_kernel(medium_scale, short_scale, sums_ref, medium_ref, short_ref):
    parts = sums_ref.shape[0]
    groups = medium_ref.shape[1]
    medium = sums_ref[:, :8, :].reshape(groups, LANES)
    medium_ref[...] = medium.T * medium_scale
    for part in range(parts):
        short_ref[:, part * LANES : (part + 1) * LANES] = (
            sums_ref[part, 8 : 8 + short_ref.shape[0]] * short_scale
        )


def params(mib):
    return pltpu.CompilerParams(vmem_limit_bytes=mib * MIB)


def cost(flops, moved):
    return pl.CostEstimate(flops=flops, bytes_accessed=moved, transcendentals=0)


def columns(rows, tile=WIDE):
    return pl.BlockSpec((rows, tile), lambda step: (0, step))


def whole(array):
    return pl.BlockSpec(array.shape, lambda step: (0,) * array.ndim)


def body(queries, products, packed_grad, packed_target, short_filter, medium_filter):
    query, product = queries[0], products[0]
    rows, channels = product.shape
    group_count = medium_filter.shape[1]
    per_group = channels // group_count
    short_count = short_filter.shape[0]
    shards, copies = lax.axis_size("seq"), lax.axis_size("dp")
    capacity = 2 * rows // shards
    slots = shards * capacity
    width = channels + rows
    chunks = channels // TILE
    steps = channels // WIDE
    table = wave_table(rows)
    forth = halves(table)
    lower = beside(forth, 0, rows)
    upper = beside(forth, rows, 2 * rows)
    first = halves(table.T[:rows] / rows)
    second = halves(table.T[rows:] / rows)
    f32, bf16 = jnp.float32, jnp.bfloat16

    with jax.named_scope("pack"):
        send = pl.pallas_call(
            lambda *refs: pack_kernel(capacity, *refs),
            in_specs=[
                pl.BlockSpec(memory_space=pltpu.VMEM),
                pl.BlockSpec(memory_space=pl.ANY),
            ],
            out_specs=pl.BlockSpec(memory_space=pl.ANY),
            scratch_shapes=[
                pltpu.VMEM((rows, channels), bf16),
                pltpu.VMEM((slots, width), bf16),
                pltpu.SemaphoreType.DMA((chunks,)),
                pltpu.SemaphoreType.DMA((chunks + 1,)),
            ],
            out_shape=jax.ShapeDtypeStruct((slots, width), bf16),
            compiler_params=params(60),
            cost_estimate=cost(2 * slots * rows * width, 8 * MIB // 2),
        )(packed_target, packed_grad[0])
    with jax.named_scope("route"):
        recv = lax.all_to_all(
            send.reshape(shards, capacity, width), "seq", split_axis=0, concat_axis=0, tiled=True
        ).reshape(slots, width)
    with jax.named_scope("halo"):
        onward = [(index, index + 1) for index in range(shards - 1)]
        prev = lax.ppermute(product, "seq", onward)
    with jax.named_scope("early"):
        hidden, spec = pl.pallas_call(
            lambda *refs: early_kernel(per_group, *refs),
            grid=(steps,),
            in_specs=[
                columns(rows),
                columns(rows),
                whole(medium_filter),
                whole(forth),
                whole(lower),
                whole(second),
            ],
            out_specs=[columns(rows), columns(2 * rows)],
            out_shape=[
                jax.ShapeDtypeStruct((rows, channels), f32),
                jax.ShapeDtypeStruct((2 * rows, channels), bf16),
            ],
            compiler_params=params(60),
            cost_estimate=cost(10**14, 12 * MIB),
        )(product, prev, medium_filter, forth, lower, second)
    with jax.named_scope("tail"):
        ending, hidden = lax.optimization_barrier((query, hidden))
        tail = lax.ppermute(ending[rows - short_count + 1 :], "seq", onward)
    with jax.named_scope("grads"):
        hgrad, sums = pl.pallas_call(
            lambda *refs: grad_kernel(per_group, *refs),
            grid=(steps,),
            in_specs=[
                pl.BlockSpec((slots, rows), lambda step: (0, channels // rows)),
                columns(slots),
                columns(rows),
                columns(2 * rows),
                columns(rows),
                columns(short_count - 1),
                columns(short_count),
                whole(upper),
                whole(first),
            ],
            out_specs=[
                columns(rows),
                pl.BlockSpec((WIDE // LANES, BLOCK_ROWS, LANES), lambda step: (step, 0, 0)),
            ],
            out_shape=[
                jax.ShapeDtypeStruct((rows, channels), bf16),
                jax.ShapeDtypeStruct((channels // LANES, BLOCK_ROWS, LANES), f32),
            ],
            compiler_params=params(60),
            cost_estimate=cost(10 * rows * 2 * rows * channels, 12 * MIB),
        )(recv, recv, hidden, spec, query, tail, short_filter, upper, first)
    with jax.named_scope("sums_seq"):
        mine = jnp.sum(lax.all_to_all(sums, "seq", 0, 0, tiled=True), axis=0)
    with jax.named_scope("own_rows"):
        part = pl.pallas_call(
            lambda *refs: own_kernel(per_group, *refs),
            grid=(steps,),
            in_specs=[columns(rows)] + [whole(medium_filter), whole(lower), whole(first)],
            out_specs=columns(rows),
            out_shape=jax.ShapeDtypeStruct((rows, channels), f32),
            compiler_params=params(60),
            cost_estimate=cost(16 * rows * 2 * rows * channels, 3 * MIB),
        )(hgrad, medium_filter, lower, first)
    with jax.named_scope("later"):
        part, leaving = lax.optimization_barrier((part, hgrad))
        following = lax.ppermute(
            leaving, "seq", [(index + 1, index) for index in range(shards - 1)]
        )
    with jax.named_scope("sums_dp"):
        spread = jnp.broadcast_to(mine[None], (copies, BLOCK_ROWS, LANES))
        mine = jnp.sum(lax.all_to_all(spread, "dp", 0, 0, tiled=True), axis=0)
    with jax.named_scope("input_grad"):
        input_grad = pl.pallas_call(
            lambda *refs: input_kernel(per_group, *refs),
            grid=(steps,),
            in_specs=[columns(rows), columns(rows)]
            + [whole(medium_filter), whole(lower), whole(upper), whole(first)],
            out_specs=columns(rows),
            out_shape=jax.ShapeDtypeStruct((rows, channels), bf16),
            compiler_params=params(60),
            cost_estimate=cost(16 * rows * 2 * rows * channels, 4 * MIB),
        )(part, following, medium_filter, lower, upper, first)
    with jax.named_scope("sums_all"):
        spread = jnp.broadcast_to(mine[None], (shards, BLOCK_ROWS, LANES))
        total = lax.all_to_all(spread, "seq", 0, 0, tiled=True)
    with jax.named_scope("finish"):
        positions = copies * shards * rows
        medium_scale = 1.0 / math.sqrt(positions * per_group)
        short_scale = 1.0 / math.sqrt(positions)
        medium_grad, short_grad = pl.pallas_call(
            lambda *refs: last_kernel(medium_scale, short_scale, *refs),
            out_shape=[
                jax.ShapeDtypeStruct((rows, group_count), f32),
                jax.ShapeDtypeStruct((short_count, channels), f32),
            ],
            compiler_params=params(8),
        )(total)
    return input_grad[None], medium_grad, short_grad


def solution(mesh):
    in_specs = (
        P("dp", "seq", None),
        P("dp", "seq", None),
        P("dp", "seq", None),
        P("dp", "seq"),
        P(),
        P(),
    )
    out_specs = (P("dp", "seq", None), P(), P())
    return jax.shard_map(body, mesh=mesh, in_specs=in_specs, out_specs=out_specs, check_vma=False)
```

```python
import math

import jax
import jax.numpy as jnp
import numpy as np
from jax import lax
from jax.experimental import pallas as pl
from jax.experimental.pallas import tpu as pltpu
from jax.sharding import PartitionSpec as P

TILE = 1024
WIDE = 2048
LANES = 128
BLOCK_ROWS = 16
MIB = 1024 * 1024


def split(value):
    high = value.astype(jnp.bfloat16)
    low = (value - high.astype(jnp.float32)).astype(jnp.bfloat16)
    return high, low


def wave_table(rows):
    size = 2 * rows
    phase = (np.arange(size)[None, :] * (2 * np.arange(rows)[:, None] + 1)) % (2 * size)
    angle = phase * (math.pi / size)
    return np.concatenate([np.cos(angle), -np.sin(angle)], axis=0)


def halves(table):
    high = table.astype(jnp.bfloat16)
    low = (table - high.astype(np.float64)).astype(jnp.bfloat16)
    return jnp.asarray(np.concatenate([high, low], axis=0))


def beside(table, start, stop):
    half = table.shape[0] // 2
    return jnp.concatenate([table[:half, start:stop], table[half:, start:stop]], axis=1)


def mm(left, right):
    return jnp.dot(left, right, preferred_element_type=jnp.float32)


def forward(table, value):
    both = mm(table, value)
    half = both.shape[0] // 2
    return both[:half] + both[half:]


def narrow(table, value):
    return mm(table, jnp.concatenate([value, value], axis=0))


def backward(table, value):
    top, rest = split(value)
    return forward(table, top) + mm(table[: table.shape[0] // 2], rest)


def halved(spec):
    half = spec.shape[0] // 2
    return spec[:half], spec[half:]


def filter_spec(taps, table, per_group, tile):
    group_count = taps.shape[1]
    channel = lax.broadcasted_iota(jnp.int32, (group_count, tile), 1) + pl.program_id(0) * tile
    group = lax.broadcasted_iota(jnp.int32, (group_count, tile), 0)
    first = group * per_group
    expand = ((channel >= first) & (channel < first + per_group)).astype(jnp.bfloat16)
    wide = mm(taps, expand).astype(jnp.bfloat16)
    return narrow(table, wide)


def delayed(query, tail, steps):
    moved = pltpu.roll(query, steps, 0)
    row = lax.broadcasted_iota(jnp.int32, query.shape, 0)
    for index in range(steps):
        source = tail.shape[0] - steps + index
        moved = jnp.where(row == index, tail[source : source + 1], moved)
    return moved


def smoothing(query, tail, short):
    moved = [query] + [delayed(query, tail, offset) for offset in range(1, short.shape[0])]
    return sum(short[offset : offset + 1] * value for offset, value in enumerate(moved)), moved


def pack_kernel(capacity, target_ref, grad_ref, out_ref, block, held, come, leave):
    rows, channels = grad_ref.shape
    slots = out_ref.shape[0]
    parts = channels // TILE
    arriving = []
    for index in range(parts):
        cut = pl.ds(index * TILE, TILE)
        arriving.append(
            pltpu.make_async_copy(grad_ref.at[:, cut], block.at[:, cut], come.at[index])
        )
        arriving[-1].start()

    def leaving(cut, index):
        return pltpu.make_async_copy(held.at[:, cut], out_ref.at[:, cut], leave.at[index])

    wide = jnp.broadcast_to(target_ref[...].astype(jnp.float32), (rows, rows))
    across = wide.astype(jnp.int32)
    down = wide.T.astype(jnp.int32)
    upper = lax.broadcasted_iota(jnp.int32, (rows, rows), 0)
    right = lax.broadcasted_iota(jnp.int32, (rows, rows), 1)
    owner = lax.div(across, rows)
    earlier = (owner == lax.div(down, rows)) & (upper < right)
    rank = jnp.sum(earlier.astype(jnp.float32), axis=0, keepdims=True).astype(jnp.int32)
    slot = owner[:1] * capacity + rank
    placing = (lax.broadcasted_iota(jnp.int32, (slots, rows), 0) == slot).astype(jnp.bfloat16)
    for index, copy in enumerate(arriving):
        cut = pl.ds(index * TILE, TILE)
        copy.wait()
        held[:, cut] = mm(placing, block[:, cut]).astype(jnp.bfloat16)
        leaving(cut, index).start()
    landing = (lax.rem(down, rows) == right).astype(jnp.bfloat16)
    held[:, channels:] = mm(placing, landing).astype(jnp.bfloat16)
    leaving(pl.ds(channels, rows), parts).start()
    for index in range(parts):
        leaving(pl.ds(index * TILE, TILE), index).wait()
    leaving(pl.ds(channels, rows), parts).wait()


def early_kernel(
    per_group,
    own_ref,
    prev_ref,
    taps_ref,
    ft_ref,
    fn_ref,
    it_ref,
    hidden_ref,
    spec_ref,
):
    spec = forward(ft_ref[...], jnp.concatenate([prev_ref[...], own_ref[...]], axis=0))
    spec_ref[...] = spec.astype(jnp.bfloat16)
    wave = filter_spec(taps_ref[...], fn_ref[...], per_group, own_ref.shape[1])
    sr, si = halved(spec)
    wr, wi = halved(wave)
    product = jnp.concatenate([sr * wr - si * wi, sr * wi + si * wr], axis=0)
    hidden_ref[...] = backward(it_ref[...], product)


def grad_kernel(
    per_group,
    land_ref,
    recv_ref,
    hidden_ref,
    spec_ref,
    query_ref,
    tail_ref,
    short_ref,
    fn_ref,
    ct_ref,
    hgrad_ref,
    sums_ref,
):
    tile = hgrad_ref.shape[1]
    groups = tile // per_group
    routed = lax.dot_general(
        land_ref[...],
        recv_ref[...],
        (((0,), (0,)), ((), ())),
        preferred_element_type=jnp.float32,
    )
    query = query_ref[...].astype(jnp.float32)
    tail = tail_ref[...].astype(jnp.float32)
    smoothed, moved = smoothing(query, tail, short_ref[...].astype(jnp.float32))
    hgrad = (routed * smoothed).astype(jnp.bfloat16)
    hgrad_ref[...] = hgrad
    sgrad = routed * hidden_ref[...]
    terms = [jnp.sum(sgrad * value, axis=0, keepdims=True) for value in moved]
    terms.append(jnp.zeros((8 - len(moved), tile), jnp.float32))
    short_terms = jnp.concatenate(terms, axis=0)
    gr, gi = halved(narrow(fn_ref[...], hgrad))
    pr, pi = halved(spec_ref[...].astype(jnp.float32))
    cross = jnp.concatenate([gr * pr + gi * pi, gi * pr - gr * pi], axis=0)
    first = lax.broadcasted_iota(jnp.int32, (tile, groups), 1) * per_group
    channel = lax.broadcasted_iota(jnp.int32, (tile, groups), 0)
    member = ((channel >= first) & (channel < first + per_group)).astype(jnp.bfloat16)
    grouped = mm(cross.astype(jnp.bfloat16), member)
    lagged = backward(ct_ref[...], grouped).T
    for part in range(tile // LANES):
        terms = short_terms[:, part * LANES : (part + 1) * LANES]
        both = jnp.concatenate([lagged[8 * part : 8 * part + 8], terms], axis=0)
        sums_ref[part] = both.astype(jnp.bfloat16)


def own_kernel(per_group, own_ref, taps_ref, fn_ref, it_ref, part_ref):
    gr, gi = halved(narrow(fn_ref[...], own_ref[...]))
    wr, wi = halved(filter_spec(taps_ref[...], fn_ref[...], per_group, own_ref.shape[1]))
    product = jnp.concatenate([gr * wr + gi * wi, gi * wr - gr * wi], axis=0)
    part_ref[...] = backward(it_ref[...], product)


def input_kernel(per_group, part_ref, next_ref, taps_ref, fn_ref, gn_ref, it_ref, out_ref):
    gr, gi = halved(narrow(gn_ref[...], next_ref[...]))
    wr, wi = halved(filter_spec(taps_ref[...], fn_ref[...], per_group, next_ref.shape[1]))
    product = jnp.concatenate([gr * wr + gi * wi, gi * wr - gr * wi], axis=0)
    out_ref[...] = (part_ref[...] + backward(it_ref[...], product)).astype(jnp.bfloat16)


def last_kernel(medium_scale, short_scale, sums_ref, medium_ref, short_ref):
    parts = sums_ref.shape[0]
    groups = medium_ref.shape[1]
    medium = sums_ref[:, :8, :].reshape(groups, LANES)
    medium_ref[...] = medium.T * medium_scale
    for part in range(parts):
        short_ref[:, part * LANES : (part + 1) * LANES] = (
            sums_ref[part, 8 : 8 + short_ref.shape[0]] * short_scale
        )


def params(mib):
    return pltpu.CompilerParams(vmem_limit_bytes=mib * MIB)


def cost(flops, moved):
    return pl.CostEstimate(flops=flops, bytes_accessed=moved, transcendentals=0)


def columns(rows, tile=WIDE):
    return pl.BlockSpec((rows, tile), lambda step: (0, step))


def whole(array):
    return pl.BlockSpec(array.shape, lambda step: (0,) * array.ndim)


def body(queries, products, packed_grad, packed_target, short_filter, medium_filter):
    query, product = queries[0], products[0]
    rows, channels = product.shape
    group_count = medium_filter.shape[1]
    per_group = channels // group_count
    short_count = short_filter.shape[0]
    shards, copies = lax.axis_size("seq"), lax.axis_size("dp")
    capacity = 2 * rows // shards
    slots = shards * capacity
    width = channels + rows
    chunks = channels // TILE
    steps = channels // WIDE
    table = wave_table(rows)
    forth = halves(table)
    lower = beside(forth, 0, rows)
    upper = beside(forth, rows, 2 * rows)
    first = halves(table.T[:rows] / rows)
    second = halves(table.T[rows:] / rows)
    f32, bf16 = jnp.float32, jnp.bfloat16

    with jax.named_scope("pack"):
        send = pl.pallas_call(
            lambda *refs: pack_kernel(capacity, *refs),
            in_specs=[
                pl.BlockSpec(memory_space=pltpu.VMEM),
                pl.BlockSpec(memory_space=pl.ANY),
            ],
            out_specs=pl.BlockSpec(memory_space=pl.ANY),
            scratch_shapes=[
                pltpu.VMEM((rows, channels), bf16),
                pltpu.VMEM((slots, width), bf16),
                pltpu.SemaphoreType.DMA((chunks,)),
                pltpu.SemaphoreType.DMA((chunks + 1,)),
            ],
            out_shape=jax.ShapeDtypeStruct((slots, width), bf16),
            compiler_params=params(60),
            cost_estimate=cost(2 * slots * rows * width, 8 * MIB // 2),
        )(packed_target, packed_grad[0])
    with jax.named_scope("route"):
        recv = lax.all_to_all(
            send.reshape(shards, capacity, width), "seq", split_axis=0, concat_axis=0, tiled=True
        ).reshape(slots, width)
    with jax.named_scope("halo"):
        onward = [(index, index + 1) for index in range(shards - 1)]
        prev = lax.ppermute(product, "seq", onward)
    with jax.named_scope("early"):
        hidden, spec = pl.pallas_call(
            lambda *refs: early_kernel(per_group, *refs),
            grid=(steps,),
            in_specs=[
                columns(rows),
                columns(rows),
                whole(medium_filter),
                whole(forth),
                whole(lower),
                whole(second),
            ],
            out_specs=[columns(rows), columns(2 * rows)],
            out_shape=[
                jax.ShapeDtypeStruct((rows, channels), f32),
                jax.ShapeDtypeStruct((2 * rows, channels), bf16),
            ],
            compiler_params=params(60),
            cost_estimate=cost(10**14, 12 * MIB),
        )(product, prev, medium_filter, forth, lower, second)
    with jax.named_scope("tail"):
        ending, hidden = lax.optimization_barrier((query, hidden))
        tail = lax.ppermute(ending[rows - short_count + 1 :], "seq", onward)
    with jax.named_scope("grads"):
        hgrad, sums = pl.pallas_call(
            lambda *refs: grad_kernel(per_group, *refs),
            grid=(steps,),
            in_specs=[
                pl.BlockSpec((slots, rows), lambda step: (0, channels // rows)),
                columns(slots),
                columns(rows),
                columns(2 * rows),
                columns(rows),
                columns(short_count - 1),
                columns(short_count),
                whole(upper),
                whole(first),
            ],
            out_specs=[
                columns(rows),
                pl.BlockSpec((WIDE // LANES, BLOCK_ROWS, LANES), lambda step: (step, 0, 0)),
            ],
            out_shape=[
                jax.ShapeDtypeStruct((rows, channels), bf16),
                jax.ShapeDtypeStruct((channels // LANES, BLOCK_ROWS, LANES), bf16),
            ],
            compiler_params=params(60),
            cost_estimate=cost(10 * rows * 2 * rows * channels, 12 * MIB),
        )(recv, recv, hidden, spec, query, tail, short_filter, upper, first)
    with jax.named_scope("sums_seq"):
        shares = lax.all_to_all(sums, "seq", 0, 0, tiled=True)
        mine = jnp.sum(shares.astype(f32), axis=0)
    with jax.named_scope("own_rows"):
        part = pl.pallas_call(
            lambda *refs: own_kernel(per_group, *refs),
            grid=(steps,),
            in_specs=[columns(rows)] + [whole(medium_filter), whole(lower), whole(first)],
            out_specs=columns(rows),
            out_shape=jax.ShapeDtypeStruct((rows, channels), f32),
            compiler_params=params(60),
            cost_estimate=cost(16 * rows * 2 * rows * channels, 3 * MIB),
        )(hgrad, medium_filter, lower, first)
    with jax.named_scope("later"):
        part, leaving = lax.optimization_barrier((part, hgrad))
        following = lax.ppermute(
            leaving, "seq", [(index + 1, index) for index in range(shards - 1)]
        )
    with jax.named_scope("sums_dp"):
        spread = jnp.broadcast_to(mine[None], (copies, BLOCK_ROWS, LANES))
        mine = jnp.sum(lax.all_to_all(spread, "dp", 0, 0, tiled=True), axis=0)
    with jax.named_scope("input_grad"):
        input_grad = pl.pallas_call(
            lambda *refs: input_kernel(per_group, *refs),
            grid=(steps,),
            in_specs=[columns(rows), columns(rows)]
            + [whole(medium_filter), whole(lower), whole(upper), whole(first)],
            out_specs=columns(rows),
            out_shape=jax.ShapeDtypeStruct((rows, channels), bf16),
            compiler_params=params(60),
            cost_estimate=cost(16 * rows * 2 * rows * channels, 4 * MIB),
        )(part, following, medium_filter, lower, upper, first)
    with jax.named_scope("sums_all"):
        spread = jnp.broadcast_to(mine[None], (shards, BLOCK_ROWS, LANES))
        total = lax.all_to_all(spread, "seq", 0, 0, tiled=True)
    with jax.named_scope("finish"):
        positions = copies * shards * rows
        medium_scale = 1.0 / math.sqrt(positions * per_group)
        short_scale = 1.0 / math.sqrt(positions)
        medium_grad, short_grad = pl.pallas_call(
            lambda *refs: last_kernel(medium_scale, short_scale, *refs),
            out_shape=[
                jax.ShapeDtypeStruct((rows, group_count), f32),
                jax.ShapeDtypeStruct((short_count, channels), f32),
            ],
            compiler_params=params(8),
        )(total)
    return input_grad[None], medium_grad, short_grad


def solution(mesh):
    in_specs = (
        P("dp", "seq", None),
        P("dp", "seq", None),
        P("dp", "seq", None),
        P("dp", "seq"),
        P(),
        P(),
    )
    out_specs = (P("dp", "seq", None), P(), P())
    return jax.shard_map(body, mesh=mesh, in_specs=in_specs, out_specs=out_specs, check_vma=False)
```
